32 devices in a mesh: seq: 4 (over z), head: 8 (over y, x, core).
Axes of the slice: x: 2, y: 2, z: 4, core: 2. Of those that a mesh axis runs over, the one named last changes fastest.
Arguments:
- queries: bfloat16 [2048, 32, 128], P(('seq', 'head')), may hold values from -6 to 6
- keys: bfloat16 [2048, 32, 128], P(('seq', 'head')), may hold values from -6 to 6
- values: bfloat16 [2048, 32, 128], P(('seq', 'head')), may hold values from -6 to 6
- out_grad: bfloat16 [2048, 32, 128], P(('seq', 'head')), may hold values from -1.5 to 1.5
- level_weights: float32 [32, 12, 2048], P('head', None, 'seq'), may hold values from 0.2 to 2
Outputs:
- query_grad: bfloat16 [2048, 32, 128], P(('seq', 'head'))
- key_grad: bfloat16 [2048, 32, 128], P(('seq', 'head'))
- value_grad: bfloat16 [2048, 32, 128], P(('seq', 'head'))
- weight_grad: float32 [32, 12, 2048], P('head', None, 'seq')
The draws below stay inside these ranges and needn't reach their ends.
All inputs are finite; a program needn't handle non-finite values.
Results may differ from the reference program's by a relative error of at most 0.0052.
Values may be sent and summed in bfloat16 or wider, within the bound.
A program may use at most 64 MiB of HBM per device.

```python
import math
import jax
import jax.numpy as jnp
from jax import lax

HEADS = 32
DK = 128
TOK_DEV = 512
TOKENS = 2048
LEVELS = 12


def steps_of(key, dims, cuts, least, largest):
    level, own = 1.0, jax.random.fold_in(key, 6)
    for dim, parts in cuts:
        steps = jnp.exp(jax.random.uniform(jax.random.fold_in(own, dim), (parts,), jnp.float32, least / len(cuts), largest / len(cuts)))
        level = level * jnp.repeat(steps, dims[dim] // parts).reshape([-1 if axis == dim else 1 for axis in range(len(dims))])
    return level


def bell_draw(stream_key, dims, scale, limit, cuts=(), held_as=jnp.bfloat16):
    factor_of = steps_of(stream_key, dims, cuts, -0.22, 0.18) if cuts else 1.0
    values = jax.random.normal(stream_key, dims, jnp.float32) * scale * factor_of
    return jnp.minimum(jnp.maximum(values, -limit), limit).astype(held_as)


def setup_inputs(seed: int = 0) -> dict:
    arg_keys = jax.random.split(jax.random.key(seed), 6)
    queries = bell_draw(arg_keys[0], (TOKENS, HEADS, DK), 1.0, 6.0, ((0, 32),))
    keys = bell_draw(arg_keys[1], (TOKENS, HEADS, DK), 1.0, 6.0, ((0, 32),))
    values = bell_draw(arg_keys[2], (TOKENS, HEADS, DK), 1.0, 6.0, ((0, 32),))
    out_grad = bell_draw(arg_keys[3], (TOKENS, HEADS, DK), 0.25, 1.5, ((0, 32),))
    level_weights = jnp.clip(jnp.exp(math.log(2.0) - 2.3025851 * jax.random.uniform(arg_keys[4], (HEADS, LEVELS, TOKENS), jnp.float32) ** steps_of(arg_keys[4], (HEADS, LEVELS, TOKENS), ((0, 8), (2, 4)), -0.2, 0.2)), 0.2, 2.0)
    return dict(queries=queries, keys=keys, values=values, out_grad=out_grad, level_weights=level_weights)


def bit_length(values, number):
    running = jnp.zeros(values.shape, jnp.int32)
    for exponent in range(number):
        running = running + (values >= 2 ** exponent).astype(jnp.int32)
    return running

def level_factors(number):
    base_scale = 1.0 / math.sqrt(DK)
    factors = [base_scale] + [base_scale * 2.0 ** (-(degree - 1) / 2.0) for degree in range(1, number)]
    return jnp.array(factors, jnp.float32)

def near_block(inputs):
    query_rows, key_rows, value_rows, grad_rows, weight_rows = inputs
    local_count = weight_rows.shape[0]
    positions = jnp.arange(TOK_DEV, dtype=jnp.int32)
    crossed = jnp.bitwise_xor(positions[:, None], positions[None, :])
    levels = bit_length(crossed, local_count - 1)
    causal = positions[None, :] <= positions[:, None]
    factors = level_factors(local_count)
    picked = jnp.take_along_axis(weight_rows.T, levels, axis=1)
    weights = jnp.where(causal, factors[levels] * picked, 0.0)
    scores = jnp.dot(query_rows, key_rows.T, preferred_element_type=jnp.float32)
    pulls = jnp.dot(grad_rows, value_rows.T, preferred_element_type=jnp.float32)
    near_scaled = (weights * scores).astype(jnp.bfloat16)
    near_pulled = (weights * pulls).astype(jnp.bfloat16)
    value_part = jnp.dot(near_scaled.T, grad_rows, preferred_element_type=jnp.float32)
    query_part = jnp.dot(near_pulled, key_rows, preferred_element_type=jnp.float32)
    key_part = jnp.dot(near_pulled.T, query_rows, preferred_element_type=jnp.float32)
    product = jnp.where(causal, scores * pulls, 0.0)
    weight_part = jnp.stack([factors[degree] * lax.optimization_barrier(jnp.sum(jnp.where(levels == degree, product, 0.0), axis=1)) for degree in range(local_count)])
    return (query_part, key_part, value_part, weight_part)

def one_head(inputs):
    queries, keys, values, out_grad, level_weights = inputs
    blocks = TOKENS // TOK_DEV
    local_count = TOK_DEV.bit_length()
    far_count = LEVELS - local_count
    query_blocks = queries.reshape(blocks, TOK_DEV, DK)
    key_blocks = keys.reshape(blocks, TOK_DEV, DK)
    value_blocks = values.reshape(blocks, TOK_DEV, DK)
    grad_blocks = out_grad.reshape(blocks, TOK_DEV, DK)
    near_weights = level_weights[:local_count].reshape(local_count, blocks, TOK_DEV).transpose(1, 0, 2)
    query_near, key_near, value_near, weight_near = lax.map(near_block, (query_blocks, key_blocks, value_blocks, grad_blocks, near_weights))
    query_wide = query_blocks.astype(jnp.float32)
    key_wide = key_blocks.astype(jnp.float32)
    value_wide = value_blocks.astype(jnp.float32)
    grad_wide = grad_blocks.astype(jnp.float32)
    factors = level_factors(LEVELS)[local_count:]
    far_weights = level_weights[local_count:].reshape(far_count, blocks, TOK_DEV)
    coefficient = factors[:, None, None] * far_weights
    pair_state = jnp.einsum('mcd,mce->mde', key_wide, value_wide, precision=lax.Precision.HIGHEST)
    scaled_grad = (coefficient[..., None] * grad_wide[None]).astype(jnp.bfloat16)
    query_state = jnp.einsum('mcd,jmce->jmde', query_wide, scaled_grad.astype(jnp.float32), precision=lax.Precision.HIGHEST)
    indices = jnp.arange(blocks, dtype=jnp.int32)
    crossed = jnp.bitwise_xor(indices[:, None], indices[None, :])
    first_bit = bit_length(crossed, far_count)
    degrees = jnp.arange(far_count, dtype=jnp.int32)[:, None, None] + 1
    lower_mask = ((first_bit[None] == degrees) & (indices[None, None, :] < indices[None, :, None])).astype(jnp.float32)
    upper_mask = ((first_bit[None] == degrees) & (indices[None, None, :] > indices[None, :, None])).astype(jnp.float32)
    lower_state = jnp.einsum('jmn,nde->jmde', lower_mask, pair_state, precision=lax.Precision.HIGHEST).astype(jnp.bfloat16)
    upper_sum = lax.optimization_barrier(jnp.sum(jnp.einsum('jmn,jnde->jmde', upper_mask, query_state, precision=lax.Precision.HIGHEST), axis=0)).astype(jnp.bfloat16)
    far_update = jnp.einsum('mce,jmde->jmcd', grad_wide, lower_state.astype(jnp.float32), precision=lax.Precision.HIGHEST)
    query_grad = (query_near + lax.optimization_barrier(jnp.sum(coefficient[..., None] * far_update, axis=0))).astype(jnp.bfloat16)
    upper_wide = upper_sum.astype(jnp.float32)
    key_grad = (key_near + jnp.einsum('mce,mde->mcd', value_wide, upper_wide, precision=lax.Precision.HIGHEST)).astype(jnp.bfloat16)
    value_grad = (value_near + jnp.einsum('mcd,mde->mce', key_wide, upper_wide, precision=lax.Precision.HIGHEST)).astype(jnp.bfloat16)
    weight_far = factors[:, None, None] * lax.optimization_barrier(jnp.sum(query_wide[None] * far_update, axis=-1))
    weight_grad = jnp.concatenate([weight_near.transpose(1, 0, 2).reshape(local_count, TOKENS), weight_far.reshape(far_count, TOKENS)], axis=0)
    return (query_grad.reshape(TOKENS, DK), key_grad.reshape(TOKENS, DK), value_grad.reshape(TOKENS, DK), weight_grad)

def reference(queries, keys, values, out_grad, level_weights):
    head_major = tuple((jnp.moveaxis(member, 1, 0) for member in (queries, keys, values, out_grad)))
    query_grad, key_grad, value_grad, weight_grad = lax.map(one_head, head_major + (level_weights,))
    return (jnp.moveaxis(query_grad, 0, 1), jnp.moveaxis(key_grad, 0, 1), jnp.moveaxis(value_grad, 0, 1), weight_grad)
```

```python
import functools
import math

import jax
import jax.numpy as jnp
from jax import lax
from jax.experimental import pallas as pl
from jax.experimental.pallas import tpu as pltpu
from jax.sharding import PartitionSpec as P

MESH = pl.DeviceIdType.MESH
TILE = 128
SIDE = 256
F32 = jnp.float32
BF16 = jnp.bfloat16


def level_factor(degree, head_width):
    base_scale = 1.0 / math.sqrt(head_width)
    if degree == 0:
        return base_scale
    return base_scale * 2.0 ** (-(degree - 1) / 2.0)


def dot(left, right):
    return jnp.dot(left, right, preferred_element_type=F32)


def dot_nt(left, right):
    return lax.dot_general(left, right, (((1,), (1,)), ((), ())), preferred_element_type=F32)


def kernel(
    peers,
    blocks,
    q_ref,
    k_ref,
    v_ref,
    g_ref,
    lw_ref,
    qo_ref,
    ko_ref,
    vo_ref,
    wg_ref,
    stage,
    send_buf,
    rows,
    out_rows,
    land,
    state_out,
    state_in,
    score_t,
    pull_t,
    scaled_t,
    pulled_t,
    level_ref,
    acc,
    acc_t,
    turned,
    send_sem,
    recv_sem,
    out_send_sem,
    out_recv_sem,
    state_send_sem,
    state_recv_sem,
):
    part, heads, width = q_ref.shape
    here = heads // peers
    toks = part * peers
    local_bits = toks.bit_length() - 1
    first_far = local_bits + 1
    far = blocks.bit_length() - 1
    tiles = toks // TILE
    tile_bits = TILE.bit_length() - 1
    sides = toks // SIDE
    me = lax.axis_index("head")
    block = lax.axis_index("seq")

    def peer(offset):
        return lax.rem(me + offset, peers)

    def source(offset):
        return lax.rem(me + peers - offset, peers)

    def block_to(offset):
        return lax.rem(block + offset, blocks)

    def block_from(offset):
        return lax.rem(block + blocks - offset, blocks)

    def part_of(index):
        return pl.ds(pl.multiple_of(index * part, part), part)

    def degree_of(one, other):
        degree = 0
        for shift in range(1, far):
            apart = lax.div(one, 2**shift) != lax.div(other, 2**shift)
            degree = degree + jnp.where(apart, 1, 0)
        return degree

    barrier = pltpu.get_barrier_semaphore()
    for offset in range(1, peers):
        pl.semaphore_signal(barrier, inc=1, device_id=(block, peer(offset)), device_id_type=MESH)
    for offset in range(1, blocks):
        pl.semaphore_signal(barrier, inc=1, device_id=(block_to(offset), me), device_id_type=MESH)

    chunk = 8
    for index, ref in enumerate((q_ref, k_ref, v_ref, g_ref)):
        for start in range(0, part, chunk):
            stage[index, pl.ds(start * heads, chunk * heads), :] = (
                ref[pl.ds(start, chunk)].astype(F32).reshape(chunk * heads, width)
            )

    pl.semaphore_wait(barrier, peers + blocks - 2)

    def input_copy(head, offset):
        return pltpu.make_async_remote_copy(
            src_ref=send_buf.at[head, offset],
            dst_ref=rows.at[head, :, part_of(me), :],
            send_sem=send_sem.at[head, offset],
            recv_sem=recv_sem.at[head, offset],
            device_id=(block, peer(offset)),
            device_id_type=MESH,
        )

    def output_copy(head, offset):
        return pltpu.make_async_remote_copy(
            src_ref=out_rows.at[head, :, part_of(peer(offset)), :],
            dst_ref=land.at[head, offset],
            send_sem=out_send_sem.at[head, offset],
            recv_sem=out_recv_sem.at[head, offset],
            device_id=(block, peer(offset)),
            device_id_type=MESH,
        )

    def state_copy(head, offset):
        other = block_to(offset)
        picked = jnp.where(other > block, 0, 1 + degree_of(block, other))
        return pltpu.make_async_remote_copy(
            src_ref=state_out.at[head, picked],
            dst_ref=state_in.at[head, offset],
            send_sem=state_send_sem.at[head, offset],
            recv_sem=state_recv_sem.at[head, offset],
            device_id=(other, me),
            device_id_type=MESH,
        )

    def send_inputs(head, carry):
        for offset in list(range(1, peers)) + [0]:
            number = peer(offset) * here + head
            for index in range(4):
                picked = stage[index, pl.ds(number, part, stride=heads), :].astype(BF16)
                if offset == 0:
                    rows[head, index, part_of(me), :] = picked
                else:
                    send_buf[head, offset, index] = picked
            if offset:
                input_copy(head, offset).start()
        return carry

    lax.fori_loop(0, here, send_inputs, 0)

    later = lax.broadcasted_iota(jnp.int32, (TILE, TILE), 1)
    earlier = lax.broadcasted_iota(jnp.int32, (TILE, TILE), 0)
    crossed = jnp.bitwise_xor(later, earlier)
    running = jnp.zeros((TILE, TILE), jnp.int32)
    for exponent in range(tile_bits):
        running = running + jnp.where(crossed >= 2**exponent, 1, 0)
    level_ref[...] = jnp.where(earlier <= later, running, -1)
    scaled_t[...] = jnp.zeros_like(scaled_t)
    pulled_t[...] = jnp.zeros_like(pulled_t)

    def near(head):
        for offset in range(1, peers):
            input_copy(head, offset).wait_recv()
        query_t = rows[head, 0].T
        key_t = rows[head, 1].T
        turned[head] = query_t
        state_out[head, 0] = dot(key_t, rows[head, 2]).astype(BF16)
        for degree in range(far):
            level = first_far + degree
            weight = level_factor(level, width) * lw_ref[head, pl.ds(level, 1), :]
            scaled = (query_t.astype(F32) * weight).astype(BF16)
            state_out[head, 1 + degree] = dot(scaled, rows[head, 3]).astype(BF16)
        for offset in range(1, blocks):
            state_copy(head, offset).start()
        for side in range(sides):
            columns = pl.ds(side * SIDE, SIDE)
            depth = pl.ds(0, (side + 1) * SIDE)
            score_t[depth, columns] = dot(
                rows[head, 1, depth, :], query_t[:, side * SIDE : (side + 1) * SIDE]
            )
            pull_t[depth, columns] = dot_nt(rows[head, 2, depth, :], rows[head, 3, columns, :])
        for column in range(tiles):
            columns = pl.ds(column * TILE, TILE)
            sums = {}
            for row in range(column):
                level = (row ^ column).bit_length() + tile_bits
                down = pl.ds(row * TILE, TILE)
                scores = score_t[down, columns]
                pulls = pull_t[down, columns]
                weight = level_factor(level, width) * lw_ref[head, pl.ds(level, 1), columns]
                scaled_t[down, columns] = (weight * scores).astype(BF16)
                pulled_t[down, columns] = (weight * pulls).astype(BF16)
                total = jnp.sum(scores * pulls, axis=0, keepdims=True)
                sums[level] = sums[level] + total if level in sums else total
            scores = score_t[columns, columns]
            pulls = pull_t[columns, columns]
            product = scores * pulls
            levels = level_ref[...]
            weights = jnp.zeros((TILE, TILE), F32)
            for level in range(tile_bits + 1):
                match = levels == level
                weight = level_factor(level, width) * lw_ref[head, pl.ds(level, 1), columns]
                weights = jnp.where(match, weight, weights)
                sums[level] = jnp.sum(jnp.where(match, product, 0.0), axis=0, keepdims=True)
            scaled_t[columns, columns] = (weights * scores).astype(BF16)
            pulled_t[columns, columns] = (weights * pulls).astype(BF16)
            for level in range(local_bits + 1):
                if level in sums:
                    wg_ref[head, pl.ds(level, 1), columns] = (
                        level_factor(level, width) * sums[level]
                    )
                else:
                    wg_ref[head, pl.ds(level, 1), columns] = jnp.zeros((1, TILE), F32)
        for side in range(sides):
            down = pl.ds(side * SIDE, SIDE)
            onward = pl.ds(side * SIDE, toks - side * SIDE)
            depth = (side + 1) * SIDE
            acc[head, 0, down, :] = dot(pulled_t[down, onward], rows[head, 0, onward, :])
            acc[head, 1, down, :] = dot(scaled_t[down, onward], rows[head, 3, onward, :])
            acc_t[head, :, down] = dot(key_t[:, :depth], pulled_t[pl.ds(0, depth), down])

    def finish(head):
        upper = jnp.zeros((width, width), F32)
        lower = [jnp.zeros((width, width), F32) for degree in range(far)]
        for offset in range(1, blocks):
            state_copy(head, offset).wait_recv()
            other = block_from(offset)
            degree_here = degree_of(block, other)
            state = state_in[head, offset].astype(F32)
            upper = upper + jnp.where(other > block, state, 0.0)
            for degree in range(far):
                chosen = jnp.logical_and(other < block, degree_here == degree)
                lower[degree] = lower[degree] + jnp.where(chosen, state, 0.0)
        upper = upper.astype(BF16)
        total_t = acc_t[head]
        wide_t = turned[head].astype(F32)
        for degree in range(far):
            level = first_far + degree
            factor = level_factor(level, width)
            update_t = dot_nt(lower[degree].astype(BF16), rows[head, 3])
            total_t = total_t + (factor * lw_ref[head, pl.ds(level, 1), :]) * update_t
            wg_ref[head, pl.ds(level, 1), :] = factor * jnp.sum(
                wide_t * update_t, axis=0, keepdims=True
            )
        out_rows[head, 0] = total_t.T.astype(BF16)
        out_rows[head, 1] = (acc[head, 0] + dot_nt(rows[head, 2], upper)).astype(BF16)
        out_rows[head, 2] = (acc[head, 1] + dot(rows[head, 1], upper)).astype(BF16)
        for offset in range(1, peers):
            output_copy(head, offset).start()

    def work(step, carry):
        @pl.when(step < here)
        def _():
            near(step)

        @pl.when(step >= 1)
        def _():
            finish(step - 1)

        return carry

    lax.fori_loop(0, here + 1, work, 0)

    def gather(head, carry):
        for offset in range(peers):
            number = source(offset) * here + head
            if offset:
                output_copy(head, offset).wait_recv()
            for index in range(3):
                if offset:
                    piece = land[head, offset, index]
                else:
                    piece = out_rows[head, index, part_of(me), :]
                stage[index, pl.ds(number, part, stride=heads), :] = piece.astype(F32)
        return carry

    lax.fori_loop(0, here, gather, 0)

    for index, ref in enumerate((qo_ref, ko_ref, vo_ref)):
        for start in range(0, part, chunk):
            ref[pl.ds(start, chunk)] = (
                stage[index, pl.ds(start * heads, chunk * heads), :]
                .reshape(chunk, heads, width)
                .astype(BF16)
            )

    def drain(head, carry):
        for offset in range(1, peers):
            input_copy(head, offset).wait_send()
            output_copy(head, offset).wait_send()
        for offset in range(1, blocks):
            state_copy(head, offset).wait_send()
        return carry

    lax.fori_loop(0, here, drain, 0)


def on_device(peers, blocks, queries, keys, values, out_grad, level_weights):
    part, heads, width = queries.shape
    here = heads // peers
    toks = part * peers
    far = blocks.bit_length() - 1
    vmem = pl.BlockSpec(memory_space=pltpu.VMEM)
    narrow = jax.ShapeDtypeStruct(queries.shape, BF16)
    dma = pltpu.SemaphoreType.DMA
    flops = here * (10 * toks * toks * width + 8 * (far + 2) * toks * width * width)
    return pl.pallas_call(
        functools.partial(kernel, peers, blocks),
        out_shape=(narrow, narrow, narrow, jax.ShapeDtypeStruct(level_weights.shape, F32)),
        in_specs=[vmem] * 5,
        out_specs=(vmem,) * 4,
        scratch_shapes=[
            pltpu.VMEM((4, part * heads, width), F32),
            pltpu.VMEM((here, peers, 4, part, width), BF16),
            pltpu.VMEM((here, 4, toks, width), BF16),
            pltpu.VMEM((here, 3, toks, width), BF16),
            pltpu.VMEM((here, peers, 3, part, width), BF16),
            pltpu.VMEM((here, far + 1, width, width), BF16),
            pltpu.VMEM((here, blocks, width, width), BF16),
            pltpu.VMEM((toks, toks), F32),
            pltpu.VMEM((toks, toks), F32),
            pltpu.VMEM((toks, toks), BF16),
            pltpu.VMEM((toks, toks), BF16),
            pltpu.VMEM((TILE, TILE), jnp.int32),
            pltpu.VMEM((here, 2, toks, width), F32),
            pltpu.VMEM((here, width, toks), F32),
            pltpu.VMEM((here, width, toks), BF16),
            dma((here, peers)),
            dma((here, peers)),
            dma((here, peers)),
            dma((here, peers)),
            dma((here, blocks)),
            dma((here, blocks)),
        ],
        compiler_params=pltpu.CompilerParams(
            collective_id=0, has_side_effects=True, vmem_limit_bytes=48 * 2**20
        ),
        cost_estimate=pl.CostEstimate(
            flops=flops, bytes_accessed=7 * part * heads * width * 2, transcendentals=0
        ),
    )(queries, keys, values, out_grad, level_weights)


def solution(mesh):
    wide = P(("seq", "head"), None, None)
    levels = P("head", None, "seq")
    return jax.shard_map(
        functools.partial(on_device, mesh.shape["head"], mesh.shape["seq"]),
        mesh=mesh,
        in_specs=(wide, wide, wide, wide, levels),
        out_specs=(wide, wide, wide, levels),
        check_vma=False,
    )
```

```python
import functools
import math

import jax
import jax.numpy as jnp
from jax import lax
from jax.experimental import pallas as pl
from jax.experimental.pallas import tpu as pltpu
from jax.sharding import PartitionSpec as P

MESH = pl.DeviceIdType.MESH
TILE = 128
SIDE = 256
F32 = jnp.float32
BF16 = jnp.bfloat16


def level_factor(degree, head_width):
    base_scale = 1.0 / math.sqrt(head_width)
    if degree == 0:
        return base_scale
    return base_scale * 2.0 ** (-(degree - 1) / 2.0)


def dot(left, right):
    return jnp.dot(left, right, preferred_element_type=F32)


def dot_nt(left, right):
    return lax.dot_general(left, right, (((1,), (1,)), ((), ())), preferred_element_type=F32)


def kernel(
    peers,
    blocks,
    q_ref,
    k_ref,
    v_ref,
    g_ref,
    lw_hbm,
    qo_ref,
    ko_ref,
    vo_ref,
    wg_ref,
    fetched,
    lw_raw,
    lw_ref,
    wg_rows,
    stage,
    send_buf,
    rows,
    out_rows,
    land,
    state_out,
    state_in,
    score_t,
    pull_t,
    scaled_t,
    pulled_t,
    level_ref,
    acc,
    acc_t,
    turned,
    send_sem,
    recv_sem,
    out_send_sem,
    out_recv_sem,
    state_send_sem,
    state_recv_sem,
    fetch_sem,
):
    part, heads, width = q_ref.shape
    here = heads // peers
    toks = part * peers
    local_bits = toks.bit_length() - 1
    first_far = local_bits + 1
    far = blocks.bit_length() - 1
    tiles = toks // TILE
    tile_bits = TILE.bit_length() - 1
    sides = toks // SIDE
    me = lax.axis_index("head")
    block = lax.axis_index("seq")

    def peer(offset):
        return lax.rem(me + offset, peers)

    def source(offset):
        return lax.rem(me + peers - offset, peers)

    def block_to(offset):
        return lax.rem(block + offset, blocks)

    def block_from(offset):
        return lax.rem(block + blocks - offset, blocks)

    def part_of(index):
        return pl.ds(pl.multiple_of(index * part, part), part)

    def degree_of(one, other):
        degree = 0
        for shift in range(1, far):
            apart = lax.div(one, 2**shift) != lax.div(other, 2**shift)
            degree = degree + jnp.where(apart, 1, 0)
        return degree

    half = part // 2
    fetches = []
    for index, ref in enumerate((k_ref, v_ref, q_ref, g_ref)):
        index = (1, 2, 0, 3)[index]
        for piece in range(2):
            span = pl.ds(piece * half, half)
            fetches.append(
                pltpu.make_async_copy(
                    ref.at[span], fetched.at[index, span], fetch_sem.at[2 * index + piece]
                )
            )
    fetch_levels = pltpu.make_async_copy(lw_hbm, lw_raw, fetch_sem.at[8])
    for copy in fetches:
        copy.start()
    fetch_levels.start()
    barrier = pltpu.get_barrier_semaphore()
    for offset in range(1, peers):
        pl.semaphore_signal(barrier, inc=1, device_id=(block, peer(offset)), device_id_type=MESH)
    for offset in range(1, blocks):
        pl.semaphore_signal(barrier, inc=1, device_id=(block_to(offset), me), device_id_type=MESH)

    later = lax.broadcasted_iota(jnp.int32, (TILE, TILE), 1)
    earlier = lax.broadcasted_iota(jnp.int32, (TILE, TILE), 0)
    crossed = jnp.bitwise_xor(later, earlier)
    running = jnp.zeros((TILE, TILE), jnp.int32)
    for exponent in range(tile_bits):
        running = running + jnp.where(crossed >= 2**exponent, 1, 0)
    level_ref[...] = jnp.where(earlier <= later, running, -1)
    scaled_t[...] = jnp.zeros_like(scaled_t)
    pulled_t[...] = jnp.zeros_like(pulled_t)

    chunk = 8
    for order, index in enumerate((1, 2, 0, 3)):
        for start in range(0, part, chunk):
            if start % half == 0:
                fetches[2 * order + start // half].wait()
            stage[index, pl.ds(start * heads, chunk * heads), :] = (
                fetched[index, pl.ds(start, chunk)].astype(F32).reshape(chunk * heads, width)
            )

    pl.semaphore_wait(barrier, peers + blocks - 2)

    def input_copy(head, offset):
        return pltpu.make_async_remote_copy(
            src_ref=send_buf.at[head, offset],
            dst_ref=rows.at[head, :, part_of(me), :],
            send_sem=send_sem.at[head, offset],
            recv_sem=recv_sem.at[head, offset],
            device_id=(block, peer(offset)),
            device_id_type=MESH,
        )

    def output_copy(head, offset):
        return pltpu.make_async_remote_copy(
            src_ref=out_rows.at[head, :, part_of(peer(offset)), :],
            dst_ref=land.at[head, offset],
            send_sem=out_send_sem.at[head, offset],
            recv_sem=out_recv_sem.at[head, offset],
            device_id=(block, peer(offset)),
            device_id_type=MESH,
        )

    def state_copy(head, offset):
        other = block_to(offset)
        picked = jnp.where(other > block, 0, 1 + degree_of(block, other))
        return pltpu.make_async_remote_copy(
            src_ref=state_out.at[head, picked],
            dst_ref=state_in.at[head, offset],
            send_sem=state_send_sem.at[head, offset],
            recv_sem=state_recv_sem.at[head, offset],
            device_id=(other, me),
            device_id_type=MESH,
        )

    def send_inputs(head, carry):
        for offset in list(range(1, peers)) + [0]:
            number = peer(offset) * here + head
            for index in range(4):
                picked = stage[index, pl.ds(number, part, stride=heads), :].astype(BF16)
                if offset == 0:
                    rows[head, index, part_of(me), :] = picked
                else:
                    send_buf[head, offset, index] = picked
            if offset:
                input_copy(head, offset).start()
        return carry

    lax.fori_loop(0, here, send_inputs, 0)
    fetch_levels.wait()
    for level in range(first_far + far):
        for head in range(here):
            lw_ref[head, pl.ds(level, 1), :] = lw_raw[level, pl.ds(head, 1), :]

    def near(head):
        for offset in range(1, peers):
            input_copy(head, offset).wait_recv()
        query_t = rows[head, 0].T
        key_t = rows[head, 1].T
        turned[head] = query_t
        state_out[head, 0] = dot(key_t, rows[head, 2]).astype(BF16)
        for degree in range(far):
            level = first_far + degree
            weight = level_factor(level, width) * lw_ref[head, pl.ds(level, 1), :]
            scaled = (query_t.astype(F32) * weight).astype(BF16)
            state_out[head, 1 + degree] = dot(scaled, rows[head, 3]).astype(BF16)
        for offset in range(1, blocks):
            state_copy(head, offset).start()
        for side in range(sides):
            columns = pl.ds(side * SIDE, SIDE)
            depth = pl.ds(0, (side + 1) * SIDE)
            score_t[depth, columns] = dot(
                rows[head, 1, depth, :], query_t[:, side * SIDE : (side + 1) * SIDE]
            )
            pull_t[depth, columns] = dot_nt(rows[head, 2, depth, :], rows[head, 3, columns, :])
        for column in range(tiles):
            columns = pl.ds(column * TILE, TILE)
            sums = {}
            for row in range(column):
                level = (row ^ column).bit_length() + tile_bits
                down = pl.ds(row * TILE, TILE)
                scores = score_t[down, columns]
                pulls = pull_t[down, columns]
                weight = level_factor(level, width) * lw_ref[head, pl.ds(level, 1), columns]
                scaled_t[down, columns] = (weight * scores).astype(BF16)
                pulled_t[down, columns] = (weight * pulls).astype(BF16)
                total = jnp.sum(scores * pulls, axis=0, keepdims=True)
                sums[level] = sums[level] + total if level in sums else total
            scores = score_t[columns, columns]
            pulls = pull_t[columns, columns]
            product = scores * pulls
            levels = level_ref[...]
            weights = jnp.zeros((TILE, TILE), F32)
            for level in range(tile_bits + 1):
                match = levels == level
                weight = level_factor(level, width) * lw_ref[head, pl.ds(level, 1), columns]
                weights = jnp.where(match, weight, weights)
                sums[level] = jnp.sum(jnp.where(match, product, 0.0), axis=0, keepdims=True)
            scaled_t[columns, columns] = (weights * scores).astype(BF16)
            pulled_t[columns, columns] = (weights * pulls).astype(BF16)
            for level in range(local_bits + 1):
                if level in sums:
                    wg_rows[head, pl.ds(level, 1), columns] = (
                        level_factor(level, width) * sums[level]
                    )
                else:
                    wg_rows[head, pl.ds(level, 1), columns] = jnp.zeros((1, TILE), F32)
        for side in range(sides):
            down = pl.ds(side * SIDE, SIDE)
            onward = pl.ds(side * SIDE, toks - side * SIDE)
            depth = (side + 1) * SIDE
            acc[head, 0, down, :] = dot(pulled_t[down, onward], rows[head, 0, onward, :])
            acc[head, 1, down, :] = dot(scaled_t[down, onward], rows[head, 3, onward, :])
            acc_t[head, :, down] = dot(key_t[:, :depth], pulled_t[pl.ds(0, depth), down])

    def finish(head):
        upper = jnp.zeros((width, width), F32)
        lower = [jnp.zeros((width, width), F32) for degree in range(far)]
        for offset in range(1, blocks):
            state_copy(head, offset).wait_recv()
            other = block_from(offset)
            degree_here = degree_of(block, other)
            state = state_in[head, offset].astype(F32)
            upper = upper + jnp.where(other > block, state, 0.0)
            for degree in range(far):
                chosen = jnp.logical_and(other < block, degree_here == degree)
                lower[degree] = lower[degree] + jnp.where(chosen, state, 0.0)
        upper = upper.astype(BF16)
        total_t = acc_t[head]
        wide_t = turned[head].astype(F32)
        for degree in range(far):
            level = first_far + degree
            factor = level_factor(level, width)
            update_t = dot_nt(lower[degree].astype(BF16), rows[head, 3])
            total_t = total_t + (factor * lw_ref[head, pl.ds(level, 1), :]) * update_t
            wg_rows[head, pl.ds(level, 1), :] = factor * jnp.sum(
                wide_t * update_t, axis=0, keepdims=True
            )
        out_rows[head, 0] = total_t.T.astype(BF16)
        out_rows[head, 1] = (acc[head, 0] + dot_nt(rows[head, 2], upper)).astype(BF16)
        out_rows[head, 2] = (acc[head, 1] + dot(rows[head, 1], upper)).astype(BF16)
        for offset in range(1, peers):
            output_copy(head, offset).start()

    def work(step, carry):
        @pl.when(step < here)
        def _():
            near(step)

        @pl.when(step >= 1)
        def _():
            finish(step - 1)

        return carry

    lax.fori_loop(0, here + 1, work, 0)
    for level in range(first_far + far):
        for head in range(here):
            lw_raw[level, pl.ds(head, 1), :] = wg_rows[head, pl.ds(level, 1), :]

    def gather(head, carry):
        for offset in range(peers):
            number = source(offset) * here + head
            if offset:
                output_copy(head, offset).wait_recv()
            for index in range(3):
                if offset:
                    piece = land[head, offset, index]
                else:
                    piece = out_rows[head, index, part_of(me), :]
                stage[index, pl.ds(number, part, stride=heads), :] = piece.astype(F32)
        return carry

    lax.fori_loop(0, here, gather, 0)

    stores = [pltpu.make_async_copy(lw_raw, wg_ref, fetch_sem.at[8])]
    stores[0].start()
    for index, ref in enumerate((qo_ref, ko_ref, vo_ref)):
        for start in range(0, part, chunk):
            fetched[index, pl.ds(start, chunk)] = (
                stage[index, pl.ds(start * heads, chunk * heads), :]
                .reshape(chunk, heads, width)
                .astype(BF16)
            )
            if (start + chunk) % half == 0:
                piece = start // half
                span = pl.ds(piece * half, half)
                copy = pltpu.make_async_copy(
                    fetched.at[index, span], ref.at[span], fetch_sem.at[2 * index + piece]
                )
                copy.start()
                stores.append(copy)
    for copy in stores:
        copy.wait()

    def drain(head, carry):
        for offset in range(1, peers):
            input_copy(head, offset).wait_send()
            output_copy(head, offset).wait_send()
        for offset in range(1, blocks):
            state_copy(head, offset).wait_send()
        return carry

    lax.fori_loop(0, here, drain, 0)


def store_kernel(*refs):
    part = refs[0].shape[0] // 4
    sem = refs[8]
    copies = []
    for index in range(3):
        for piece in range(4):
            span = pl.ds(piece * part, part)
            copies.append(
                pltpu.make_async_copy(
                    refs[index].at[span], refs[4 + index].at[span], sem.at[4 * index + piece]
                )
            )
    copies.append(pltpu.make_async_copy(refs[3], refs[7], sem.at[12]))
    for copy in copies:
        copy.start()
    for copy in copies:
        copy.wait()


def on_device(peers, blocks, queries, keys, values, out_grad, level_weights):
    part, heads, width = queries.shape
    here = heads // peers
    toks = part * peers
    far = blocks.bit_length() - 1
    narrow = jax.ShapeDtypeStruct(queries.shape, BF16)
    dma = pltpu.SemaphoreType.DMA
    flops = here * (10 * toks * toks * width + 8 * (far + 2) * toks * width * width)
    hbm = pl.BlockSpec(memory_space=pltpu.HBM)
    turned_levels = jnp.transpose(level_weights, (1, 0, 2))
    shapes = (narrow, narrow, narrow, jax.ShapeDtypeStruct(turned_levels.shape, F32))
    results = pl.pallas_call(
        functools.partial(kernel, peers, blocks),
        out_shape=shapes,
        in_specs=[hbm] * 5,
        out_specs=(hbm,) * 4,
        scratch_shapes=[
            pltpu.VMEM((4, part, heads, width), BF16),
            pltpu.VMEM(turned_levels.shape, F32),
            pltpu.VMEM(level_weights.shape, F32),
            pltpu.VMEM(level_weights.shape, F32),
            pltpu.VMEM((4, part * heads, width), F32),
            pltpu.VMEM((here, peers, 4, part, width), BF16),
            pltpu.VMEM((here, 4, toks, width), BF16),
            pltpu.VMEM((here, 3, toks, width), BF16),
            pltpu.VMEM((here, peers, 3, part, width), BF16),
            pltpu.VMEM((here, far + 1, width, width), BF16),
            pltpu.VMEM((here, blocks, width, width), BF16),
            pltpu.VMEM((toks, toks), F32),
            pltpu.VMEM((toks, toks), F32),
            pltpu.VMEM((toks, toks), BF16),
            pltpu.VMEM((toks, toks), BF16),
            pltpu.VMEM((TILE, TILE), jnp.int32),
            pltpu.VMEM((here, 2, toks, width), F32),
            pltpu.VMEM((here, width, toks), F32),
            pltpu.VMEM((here, width, toks), BF16),
            dma((here, peers)),
            dma((here, peers)),
            dma((here, peers)),
            dma((here, peers)),
            dma((here, blocks)),
            dma((here, blocks)),
            dma((9,)),
        ],
        compiler_params=pltpu.CompilerParams(
            collective_id=0, has_side_effects=True, vmem_limit_bytes=58 * 2**20
        ),
        cost_estimate=pl.CostEstimate(
            flops=flops, bytes_accessed=7 * part * heads * width * 2, transcendentals=0
        ),
    )(queries, keys, values, out_grad, turned_levels)
    stored = pl.pallas_call(
        store_kernel,
        out_shape=shapes,
        in_specs=[hbm] * 4,
        out_specs=(hbm,) * 4,
        scratch_shapes=[dma((13,))],
        compiler_params=pltpu.CompilerParams(vmem_limit_bytes=58 * 2**20),
    )(*results)
    return stored[:3] + (jnp.transpose(stored[3], (1, 0, 2)),)


def solution(mesh):
    wide = P(("seq", "head"), None, None)
    levels = P("head", None, "seq")
    return jax.shard_map(
        functools.partial(on_device, mesh.shape["head"], mesh.shape["seq"]),
        mesh=mesh,
        in_specs=(wide, wide, wide, wide, levels),
        out_specs=(wide, wide, wide, levels),
        check_vma=False,
    )
```

```python
import functools
import math

import jax
import jax.numpy as jnp
from jax import lax
from jax.experimental import pallas as pl
from jax.experimental.pallas import tpu as pltpu
from jax.sharding import PartitionSpec as P

MESH = pl.DeviceIdType.MESH
TILE = 128
SIDE = 256
F32 = jnp.float32
BF16 = jnp.bfloat16


def level_factor(degree, head_width):
    base_scale = 1.0 / math.sqrt(head_width)
    if degree == 0:
        return base_scale
    return base_scale * 2.0 ** (-(degree - 1) / 2.0)


def dot(left, right):
    return jnp.dot(left, right, preferred_element_type=F32)


def dot_nt(left, right):
    return lax.dot_general(left, right, (((1,), (1,)), ((), ())), preferred_element_type=F32)


def kernel(
    peers,
    blocks,
    q_ref,
    k_ref,
    v_ref,
    g_ref,
    lw_hbm,
    qo_ref,
    ko_ref,
    vo_ref,
    wg_ref,
    fetched,
    lw_raw,
    lw_ref,
    wg_rows,
    stage,
    send_buf,
    rows,
    out_rows,
    land,
    state_out,
    state_in,
    score_t,
    pull_t,
    scaled_t,
    pulled_t,
    level_ref,
    acc,
    acc_t,
    turned,
    send_sem,
    recv_sem,
    out_send_sem,
    out_recv_sem,
    state_send_sem,
    state_recv_sem,
    fetch_sem,
):
    part, heads, width = q_ref.shape
    here = heads // peers
    toks = part * peers
    local_bits = toks.bit_length() - 1
    first_far = local_bits + 1
    far = blocks.bit_length() - 1
    tiles = toks // TILE
    tile_bits = TILE.bit_length() - 1
    sides = toks // SIDE
    me = lax.axis_index("head")
    block = lax.axis_index("seq")

    def peer(offset):
        return lax.rem(me + offset, peers)

    def source(offset):
        return lax.rem(me + peers - offset, peers)

    def block_to(offset):
        return lax.rem(block + offset, blocks)

    def block_from(offset):
        return lax.rem(block + blocks - offset, blocks)

    def part_of(index):
        return pl.ds(pl.multiple_of(index * part, part), part)

    def degree_of(one, other):
        degree = 0
        for shift in range(1, far):
            apart = lax.div(one, 2**shift) != lax.div(other, 2**shift)
            degree = degree + jnp.where(apart, 1, 0)
        return degree

    half = part // 2
    fetches = []
    for index, ref in enumerate((k_ref, v_ref, q_ref, g_ref)):
        index = (1, 2, 0, 3)[index]
        for piece in range(2):
            span = pl.ds(piece * half, half)
            fetches.append(
                pltpu.make_async_copy(
                    ref.at[span], fetched.at[index, span], fetch_sem.at[2 * index + piece]
                )
            )
    fetch_levels = pltpu.make_async_copy(lw_hbm, lw_raw, fetch_sem.at[8])
    for copy in fetches:
        copy.start()
    fetch_levels.start()
    barrier = pltpu.get_barrier_semaphore()
    for offset in range(1, peers):
        pl.semaphore_signal(barrier, inc=1, device_id=(block, peer(offset)), device_id_type=MESH)
    for offset in range(1, blocks):
        pl.semaphore_signal(barrier, inc=1, device_id=(block_to(offset), me), device_id_type=MESH)

    later = lax.broadcasted_iota(jnp.int32, (TILE, TILE), 1)
    earlier = lax.broadcasted_iota(jnp.int32, (TILE, TILE), 0)
    crossed = jnp.bitwise_xor(later, earlier)
    running = jnp.zeros((TILE, TILE), jnp.int32)
    for exponent in range(tile_bits):
        running = running + jnp.where(crossed >= 2**exponent, 1, 0)
    level_ref[...] = jnp.where(earlier <= later, running, -1)
    scaled_t[...] = jnp.zeros_like(scaled_t)
    pulled_t[...] = jnp.zeros_like(pulled_t)

    chunk = 8
    for order, index in enumerate((1, 2, 0, 3)):
        for start in range(0, part, chunk):
            if start % half == 0:
                fetches[2 * order + start // half].wait()
            stage[index, pl.ds(start * heads, chunk * heads), :] = (
                fetched[index, pl.ds(start, chunk)].astype(F32).reshape(chunk * heads, width)
            )

    pl.semaphore_wait(barrier, peers + blocks - 2)

    def input_copy(head, offset):
        return pltpu.make_async_remote_copy(
            src_ref=send_buf.at[head, offset],
            dst_ref=rows.at[head, :, part_of(me), :],
            send_sem=send_sem.at[head, offset],
            recv_sem=recv_sem.at[head, offset],
            device_id=(block, peer(offset)),
            device_id_type=MESH,
        )

    def output_copy(head, offset):
        return pltpu.make_async_remote_copy(
            src_ref=out_rows.at[head, :, part_of(peer(offset)), :],
            dst_ref=land.at[head, offset],
            send_sem=out_send_sem.at[head, offset],
            recv_sem=out_recv_sem.at[head, offset],
            device_id=(block, peer(offset)),
            device_id_type=MESH,
        )

    def state_copy(head, offset):
        other = block_to(offset)
        picked = jnp.where(other > block, 0, 1 + degree_of(block, other))
        return pltpu.make_async_remote_copy(
            src_ref=state_out.at[head, picked],
            dst_ref=state_in.at[head, offset],
            send_sem=state_send_sem.at[head, offset],
            recv_sem=state_recv_sem.at[head, offset],
            device_id=(other, me),
            device_id_type=MESH,
        )

    def send_inputs(head, carry):
        for offset in list(range(1, peers)) + [0]:
            number = peer(offset) * here + head
            for index in range(4):
                picked = stage[index, pl.ds(number, part, stride=heads), :].astype(BF16)
                if offset == 0:
                    rows[head, index, part_of(me), :] = picked
                else:
                    send_buf[head, offset, index] = picked
            if offset:
                input_copy(head, offset).start()
        return carry

    lax.fori_loop(0, here, send_inputs, 0)
    fetch_levels.wait()
    for level in range(first_far + far):
        for head in range(here):
            lw_ref[head, pl.ds(level, 1), :] = lw_raw[level, pl.ds(head, 1), :]

    def send_outputs(head, carry):
        for offset in range(1, peers):
            output_copy(head, offset).start()
        return carry

    def near(head):
        for offset in range(1, peers):
            input_copy(head, offset).wait_recv()

        @pl.when(head == here - 1)
        def _():
            lax.fori_loop(0, max(here - 2, 0), send_outputs, 0)

        query_t = rows[head, 0].T
        key_t = rows[head, 1].T
        turned[head] = query_t
        state_out[head, 0] = dot(key_t, rows[head, 2]).astype(BF16)
        for degree in range(far):
            level = first_far + degree
            weight = level_factor(level, width) * lw_ref[head, pl.ds(level, 1), :]
            scaled = (query_t.astype(F32) * weight).astype(BF16)
            state_out[head, 1 + degree] = dot(scaled, rows[head, 3]).astype(BF16)
        for offset in range(1, blocks):
            state_copy(head, offset).start()
        for side in range(sides):
            columns = pl.ds(side * SIDE, SIDE)
            depth = pl.ds(0, (side + 1) * SIDE)
            score_t[depth, columns] = dot(
                rows[head, 1, depth, :], query_t[:, side * SIDE : (side + 1) * SIDE]
            )
            pull_t[depth, columns] = dot_nt(rows[head, 2, depth, :], rows[head, 3, columns, :])
        for column in range(tiles):
            columns = pl.ds(column * TILE, TILE)
            sums = {}
            for row in range(column):
                level = (row ^ column).bit_length() + tile_bits
                down = pl.ds(row * TILE, TILE)
                scores = score_t[down, columns]
                pulls = pull_t[down, columns]
                weight = level_factor(level, width) * lw_ref[head, pl.ds(level, 1), columns]
                scaled_t[down, columns] = (weight * scores).astype(BF16)
                pulled_t[down, columns] = (weight * pulls).astype(BF16)
                total = jnp.sum(scores * pulls, axis=0, keepdims=True)
                sums[level] = sums[level] + total if level in sums else total
            scores = score_t[columns, columns]
            pulls = pull_t[columns, columns]
            product = scores * pulls
            levels = level_ref[...]
            weights = jnp.zeros((TILE, TILE), F32)
            for level in range(tile_bits + 1):
                match = levels == level
                weight = level_factor(level, width) * lw_ref[head, pl.ds(level, 1), columns]
                weights = jnp.where(match, weight, weights)
                sums[level] = jnp.sum(jnp.where(match, product, 0.0), axis=0, keepdims=True)
            scaled_t[columns, columns] = (weights * scores).astype(BF16)
            pulled_t[columns, columns] = (weights * pulls).astype(BF16)
            for level in range(local_bits + 1):
                if level in sums:
                    wg_rows[head, pl.ds(level, 1), columns] = (
                        level_factor(level, width) * sums[level]
                    )
                else:
                    wg_rows[head, pl.ds(level, 1), columns] = jnp.zeros((1, TILE), F32)
        for side in range(sides):
            down = pl.ds(side * SIDE, SIDE)
            onward = pl.ds(side * SIDE, toks - side * SIDE)
            depth = (side + 1) * SIDE
            acc[head, 0, down, :] = dot(pulled_t[down, onward], rows[head, 0, onward, :])
            acc[head, 1, down, :] = dot(scaled_t[down, onward], rows[head, 3, onward, :])
            acc_t[head, :, down] = dot(key_t[:, :depth], pulled_t[pl.ds(0, depth), down])

    def finish(head):
        upper = jnp.zeros((width, width), F32)
        lower = [jnp.zeros((width, width), F32) for degree in range(far)]
        for offset in range(1, blocks):
            state_copy(head, offset).wait_recv()
            other = block_from(offset)
            degree_here = degree_of(block, other)
            state = state_in[head, offset].astype(F32)
            upper = upper + jnp.where(other > block, state, 0.0)
            for degree in range(far):
                chosen = jnp.logical_and(other < block, degree_here == degree)
                lower[degree] = lower[degree] + jnp.where(chosen, state, 0.0)
        upper = upper.astype(BF16)
        total_t = acc_t[head]
        wide_t = turned[head].astype(F32)
        for degree in range(far):
            level = first_far + degree
            factor = level_factor(level, width)
            update_t = dot_nt(lower[degree].astype(BF16), rows[head, 3])
            total_t = total_t + (factor * lw_ref[head, pl.ds(level, 1), :]) * update_t
            wg_rows[head, pl.ds(level, 1), :] = factor * jnp.sum(
                wide_t * update_t, axis=0, keepdims=True
            )
        out_rows[head, 0] = total_t.T.astype(BF16)
        out_rows[head, 1] = (acc[head, 0] + dot_nt(rows[head, 2], upper)).astype(BF16)
        out_rows[head, 2] = (acc[head, 1] + dot(rows[head, 1], upper)).astype(BF16)

        @pl.when(head >= here - 2)
        def _():
            send_outputs(head, 0)

    def work(step, carry):
        @pl.when(step < here)
        def _():
            near(step)

        @pl.when(step >= 1)
        def _():
            finish(step - 1)

        return carry

    lax.fori_loop(0, here + 1, work, 0)
    for level in range(first_far + far):
        for head in range(here):
            lw_raw[level, pl.ds(head, 1), :] = wg_rows[head, pl.ds(level, 1), :]

    def gather(head, carry):
        for offset in range(peers):
            number = source(offset) * here + head
            if offset:
                output_copy(head, offset).wait_recv()
            for index in range(3):
                if offset:
                    piece = land[head, offset, index]
                else:
                    piece = out_rows[head, index, part_of(me), :]
                stage[index, pl.ds(number, part, stride=heads), :] = piece.astype(F32)
        return carry

    lax.fori_loop(0, here, gather, 0)

    stores = [pltpu.make_async_copy(lw_raw, wg_ref, fetch_sem.at[8])]
    stores[0].start()
    for index, ref in enumerate((qo_ref, ko_ref, vo_ref)):
        for start in range(0, part, chunk):
            fetched[index, pl.ds(start, chunk)] = (
                stage[index, pl.ds(start * heads, chunk * heads), :]
                .reshape(chunk, heads, width)
                .astype(BF16)
            )
            if (start + chunk) % half == 0:
                piece = start // half
                span = pl.ds(piece * half, half)
                copy = pltpu.make_async_copy(
                    fetched.at[index, span], ref.at[span], fetch_sem.at[2 * index + piece]
                )
                copy.start()
                stores.append(copy)
    for copy in stores:
        copy.wait()

    def drain(head, carry):
        for offset in range(1, peers):
            input_copy(head, offset).wait_send()
            output_copy(head, offset).wait_send()
        for offset in range(1, blocks):
            state_copy(head, offset).wait_send()
        return carry

    lax.fori_loop(0, here, drain, 0)


def store_kernel(*refs):
    sources, targets, held, held_levels, sem = refs[:4], refs[4:8], refs[8], refs[9], refs[10]
    part = held.shape[1] // 2
    routes = [(sources[3], held_levels, targets[3])]
    for index in range(3):
        for piece in range(2):
            span = pl.ds(piece * part, part)
            routes.append(
                (sources[index].at[span], held.at[index, span], targets[index].at[span])
            )
    loads = [
        pltpu.make_async_copy(origin, middle, sem.at[0, number])
        for number, (origin, middle, target) in enumerate(routes)
    ]
    stores = [
        pltpu.make_async_copy(middle, target, sem.at[1, number])
        for number, (origin, middle, target) in enumerate(routes)
    ]
    for copy in loads:
        copy.start()
    for load, store in zip(loads, stores):
        load.wait()
        store.start()
    for copy in stores:
        copy.wait()


def on_device(peers, blocks, queries, keys, values, out_grad, level_weights):
    part, heads, width = queries.shape
    here = heads // peers
    toks = part * peers
    far = blocks.bit_length() - 1
    narrow = jax.ShapeDtypeStruct(queries.shape, BF16)
    dma = pltpu.SemaphoreType.DMA
    flops = here * (10 * toks * toks * width + 8 * (far + 2) * toks * width * width)
    hbm = pl.BlockSpec(memory_space=pltpu.HBM)
    turned_levels = jnp.transpose(level_weights, (1, 0, 2))
    shapes = (narrow, narrow, narrow, jax.ShapeDtypeStruct(turned_levels.shape, F32))
    results = pl.pallas_call(
        functools.partial(kernel, peers, blocks),
        out_shape=shapes,
        in_specs=[hbm] * 5,
        out_specs=(hbm,) * 4,
        scratch_shapes=[
            pltpu.VMEM((4, part, heads, width), BF16),
            pltpu.VMEM(turned_levels.shape, F32),
            pltpu.VMEM(level_weights.shape, F32),
            pltpu.VMEM(level_weights.shape, F32),
            pltpu.VMEM((4, part * heads, width), F32),
            pltpu.VMEM((here, peers, 4, part, width), BF16),
            pltpu.VMEM((here, 4, toks, width), BF16),
            pltpu.VMEM((here, 3, toks, width), BF16),
            pltpu.VMEM((here, peers, 3, part, width), BF16),
            pltpu.VMEM((here, far + 1, width, width), BF16),
            pltpu.VMEM((here, blocks, width, width), BF16),
            pltpu.VMEM((toks, toks), F32),
            pltpu.VMEM((toks, toks), F32),
            pltpu.VMEM((toks, toks), BF16),
            pltpu.VMEM((toks, toks), BF16),
            pltpu.VMEM((TILE, TILE), jnp.int32),
            pltpu.VMEM((here, 2, toks, width), F32),
            pltpu.VMEM((here, width, toks), F32),
            pltpu.VMEM((here, width, toks), BF16),
            dma((here, peers)),
            dma((here, peers)),
            dma((here, peers)),
            dma((here, peers)),
            dma((here, blocks)),
            dma((here, blocks)),
            dma((9,)),
        ],
        compiler_params=pltpu.CompilerParams(
            collective_id=0, has_side_effects=True, vmem_limit_bytes=58 * 2**20
        ),
        cost_estimate=pl.CostEstimate(
            flops=flops, bytes_accessed=7 * part * heads * width * 2, transcendentals=0
        ),
    )(queries, keys, values, out_grad, turned_levels)
    stored = pl.pallas_call(
        store_kernel,
        out_shape=shapes,
        in_specs=[hbm] * 4,
        out_specs=(hbm,) * 4,
        scratch_shapes=[
            pltpu.VMEM((3, part, heads, width), BF16),
            pltpu.VMEM(turned_levels.shape, F32),
            dma((2, 7)),
        ],
        compiler_params=pltpu.CompilerParams(vmem_limit_bytes=58 * 2**20),
    )(*results)
    return stored[:3] + (jnp.transpose(stored[3], (1, 0, 2)),)


def solution(mesh):
    wide = P(("seq", "head"), None, None)
    levels = P("head", None, "seq")
    return jax.shard_map(
        functools.partial(on_device, mesh.shape["head"], mesh.shape["seq"]),
        mesh=mesh,
        in_specs=(wide, wide, wide, wide, levels),
        out_specs=(wide, wide, wide, levels),
        check_vma=False,
    )
```

```python
import functools
import math

import jax
import jax.numpy as jnp
from jax import lax
from jax.experimental import pallas as pl
from jax.experimental.pallas import tpu as pltpu
from jax.sharding import PartitionSpec as P

MESH = pl.DeviceIdType.MESH
TILE = 128
SIDE = 256
F32 = jnp.float32
BF16 = jnp.bfloat16


def level_factor(degree, head_width):
    base_scale = 1.0 / math.sqrt(head_width)
    if degree == 0:
        return base_scale
    return base_scale * 2.0 ** (-(degree - 1) / 2.0)


def dot(left, right):
    return jnp.dot(left, right, preferred_element_type=F32)


def dot_nt(left, right):
    return lax.dot_general(left, right, (((1,), (1,)), ((), ())), preferred_element_type=F32)


def kernel(
    peers,
    blocks,
    q_ref,
    k_ref,
    v_ref,
    g_ref,
    lw_hbm,
    qo_ref,
    ko_ref,
    vo_ref,
    wg_ref,
    fetched,
    lw_raw,
    lw_ref,
    wg_rows,
    stage,
    send_buf,
    rows,
    out_rows,
    land,
    state_out,
    state_in,
    score_t,
    pull_t,
    scaled_t,
    pulled_t,
    level_ref,
    acc,
    acc_t,
    turned,
    send_sem,
    recv_sem,
    out_send_sem,
    out_recv_sem,
    state_send_sem,
    state_recv_sem,
    fetch_sem,
):
    part, heads, width = q_ref.shape
    here = heads // peers
    toks = part * peers
    local_bits = toks.bit_length() - 1
    first_far = local_bits + 1
    far = blocks.bit_length() - 1
    tiles = toks // TILE
    tile_bits = TILE.bit_length() - 1
    sides = toks // SIDE
    me = lax.axis_index("head")
    block = lax.axis_index("seq")

    def peer(offset):
        return lax.rem(me + offset, peers)

    def source(offset):
        return lax.rem(me + peers - offset, peers)

    def block_to(offset):
        return lax.rem(block + offset, blocks)

    def block_from(offset):
        return lax.rem(block + blocks - offset, blocks)

    def part_of(index):
        return pl.ds(pl.multiple_of(index * part, part), part)

    def degree_of(one, other):
        degree = 0
        for shift in range(1, far):
            apart = lax.div(one, 2**shift) != lax.div(other, 2**shift)
            degree = degree + jnp.where(apart, 1, 0)
        return degree

    half = part // 2
    fetches = []
    for index, ref in enumerate((k_ref, v_ref, q_ref, g_ref)):
        index = (1, 2, 0, 3)[index]
        for piece in range(2):
            span = pl.ds(piece * half, half)
            fetches.append(
                pltpu.make_async_copy(
                    ref.at[span], fetched.at[index, span], fetch_sem.at[2 * index + piece]
                )
            )
    fetch_levels = pltpu.make_async_copy(lw_hbm, lw_raw, fetch_sem.at[8])
    for copy in fetches:
        copy.start()
    fetch_levels.start()
    barrier = pltpu.get_barrier_semaphore()
    for offset in range(1, peers):
        pl.semaphore_signal(barrier, inc=1, device_id=(block, peer(offset)), device_id_type=MESH)
    for offset in range(1, blocks):
        pl.semaphore_signal(barrier, inc=1, device_id=(block_to(offset), me), device_id_type=MESH)

    later = lax.broadcasted_iota(jnp.int32, (TILE, TILE), 1)
    earlier = lax.broadcasted_iota(jnp.int32, (TILE, TILE), 0)
    crossed = jnp.bitwise_xor(later, earlier)
    running = jnp.zeros((TILE, TILE), jnp.int32)
    for exponent in range(tile_bits):
        running = running + jnp.where(crossed >= 2**exponent, 1, 0)
    level_ref[...] = jnp.where(earlier <= later, running, -1)
    scaled_t[...] = jnp.zeros_like(scaled_t)
    pulled_t[...] = jnp.zeros_like(pulled_t)

    chunk = 8
    for order, index in enumerate((1, 2, 0, 3)):
        for start in range(0, part, chunk):
            if start % half == 0:
                fetches[2 * order + start // half].wait()
            stage[index, pl.ds(start * heads, chunk * heads), :] = (
                fetched[index, pl.ds(start, chunk)].astype(F32).reshape(chunk * heads, width)
            )

    pl.semaphore_wait(barrier, peers + blocks - 2)

    def input_copy(head, offset):
        return pltpu.make_async_remote_copy(
            src_ref=send_buf.at[head, offset],
            dst_ref=rows.at[head, :, part_of(me), :],
            send_sem=send_sem.at[head, offset],
            recv_sem=recv_sem.at[head, offset],
            device_id=(block, peer(offset)),
            device_id_type=MESH,
        )

    def output_copy(head, offset):
        return pltpu.make_async_remote_copy(
            src_ref=out_rows.at[head, :, part_of(peer(offset)), :],
            dst_ref=land.at[head, offset],
            send_sem=out_send_sem.at[head, offset],
            recv_sem=out_recv_sem.at[head, offset],
            device_id=(block, peer(offset)),
            device_id_type=MESH,
        )

    def state_copy(head, offset):
        other = block_to(offset)
        picked = jnp.where(other > block, 0, 1 + degree_of(block, other))
        return pltpu.make_async_remote_copy(
            src_ref=state_out.at[head, picked],
            dst_ref=state_in.at[head, offset],
            send_sem=state_send_sem.at[head, offset],
            recv_sem=state_recv_sem.at[head, offset],
            device_id=(other, me),
            device_id_type=MESH,
        )

    def send_inputs(head, carry):
        for offset in list(range(1, peers)) + [0]:
            number = peer(offset) * here + head
            for index in range(4):
                picked = stage[index, pl.ds(number, part, stride=heads), :].astype(BF16)
                if offset == 0:
                    rows[head, index, part_of(me), :] = picked
                else:
                    send_buf[head, offset, index] = picked
            if offset:
                input_copy(head, offset).start()
        return carry

    lax.fori_loop(0, here, send_inputs, 0)
    fetch_levels.wait()
    for level in range(first_far + far):
        for head in range(here):
            lw_ref[head, pl.ds(level, 1), :] = lw_raw[level, pl.ds(head, 1), :]

    def states(head):
        for offset in range(1, peers):
            input_copy(head, offset).wait_recv()
        query_t = rows[head, 0].T
        key_t = rows[head, 1].T
        turned[head, 0] = query_t
        turned[head, 1] = key_t
        state_out[head, 0] = dot(key_t, rows[head, 2]).astype(BF16)
        for degree in range(far):
            level = first_far + degree
            weight = level_factor(level, width) * lw_ref[head, pl.ds(level, 1), :]
            scaled = (query_t.astype(F32) * weight).astype(BF16)
            state_out[head, 1 + degree] = dot(scaled, rows[head, 3]).astype(BF16)
        for offset in range(1, blocks):
            state_copy(head, offset).start()

    def near(head):
        for side in range(sides):
            columns = pl.ds(side * SIDE, SIDE)
            depth = pl.ds(0, (side + 1) * SIDE)
            score_t[depth, columns] = dot(
                rows[head, 1, depth, :], turned[head, 0, :, columns]
            )
            pull_t[depth, columns] = dot_nt(rows[head, 2, depth, :], rows[head, 3, columns, :])
        for column in range(tiles):
            columns = pl.ds(column * TILE, TILE)
            sums = {}
            for row in range(column):
                level = (row ^ column).bit_length() + tile_bits
                down = pl.ds(row * TILE, TILE)
                scores = score_t[down, columns]
                pulls = pull_t[down, columns]
                weight = level_factor(level, width) * lw_ref[head, pl.ds(level, 1), columns]
                scaled_t[down, columns] = (weight * scores).astype(BF16)
                pulled_t[down, columns] = (weight * pulls).astype(BF16)
                total = jnp.sum(scores * pulls, axis=0, keepdims=True)
                sums[level] = sums[level] + total if level in sums else total
            scores = score_t[columns, columns]
            pulls = pull_t[columns, columns]
            product = scores * pulls
            levels = level_ref[...]
            weights = jnp.zeros((TILE, TILE), F32)
            for level in range(tile_bits + 1):
                match = levels == level
                weight = level_factor(level, width) * lw_ref[head, pl.ds(level, 1), columns]
                weights = jnp.where(match, weight, weights)
                sums[level] = jnp.sum(jnp.where(match, product, 0.0), axis=0, keepdims=True)
            scaled_t[columns, columns] = (weights * scores).astype(BF16)
            pulled_t[columns, columns] = (weights * pulls).astype(BF16)
            for level in range(local_bits + 1):
                if level in sums:
                    wg_rows[head, pl.ds(level, 1), columns] = (
                        level_factor(level, width) * sums[level]
                    )
                else:
                    wg_rows[head, pl.ds(level, 1), columns] = jnp.zeros((1, TILE), F32)
        for side in range(sides):
            down = pl.ds(side * SIDE, SIDE)
            onward = pl.ds(side * SIDE, toks - side * SIDE)
            depth = (side + 1) * SIDE
            acc[head, 0, down, :] = dot(pulled_t[down, onward], rows[head, 0, onward, :])
            acc[head, 1, down, :] = dot(scaled_t[down, onward], rows[head, 3, onward, :])
            acc_t[head, :, down] = dot(
                turned[head, 1, :, pl.ds(0, depth)], pulled_t[pl.ds(0, depth), down]
            )

    def finish(head):
        upper = jnp.zeros((width, width), F32)
        lower = [jnp.zeros((width, width), F32) for degree in range(far)]
        for offset in range(1, blocks):
            state_copy(head, offset).wait_recv()
            other = block_from(offset)
            degree_here = degree_of(block, other)
            state = state_in[head, offset].astype(F32)
            upper = upper + jnp.where(other > block, state, 0.0)
            for degree in range(far):
                chosen = jnp.logical_and(other < block, degree_here == degree)
                lower[degree] = lower[degree] + jnp.where(chosen, state, 0.0)
        upper = upper.astype(BF16)
        total_t = acc_t[head]
        wide_t = turned[head, 0].astype(F32)
        for degree in range(far):
            level = first_far + degree
            factor = level_factor(level, width)
            update_t = dot_nt(lower[degree].astype(BF16), rows[head, 3])
            total_t = total_t + (factor * lw_ref[head, pl.ds(level, 1), :]) * update_t
            wg_rows[head, pl.ds(level, 1), :] = factor * jnp.sum(
                wide_t * update_t, axis=0, keepdims=True
            )
        out_rows[head, 0] = total_t.T.astype(BF16)
        out_rows[head, 1] = (acc[head, 0] + dot_nt(rows[head, 2], upper)).astype(BF16)
        out_rows[head, 2] = (acc[head, 1] + dot(rows[head, 1], upper)).astype(BF16)
        for offset in range(1, peers):
            output_copy(head, offset).start()

    def work(step, carry):
        @pl.when(step < here)
        def _():
            states(step)

        @pl.when(step >= 1)
        def _():
            finish(step - 1)

        @pl.when(step < here)
        def _():
            near(step)

        return carry

    lax.fori_loop(0, here + 1, work, 0)
    for level in range(first_far + far):
        for head in range(here):
            lw_raw[level, pl.ds(head, 1), :] = wg_rows[head, pl.ds(level, 1), :]

    def gather(head, carry):
        for offset in range(peers):
            number = source(offset) * here + head
            if offset:
                output_copy(head, offset).wait_recv()
            for index in range(3):
                if offset:
                    piece = land[head, offset, index]
                else:
                    piece = out_rows[head, index, part_of(me), :]
                stage[index, pl.ds(number, part, stride=heads), :] = piece.astype(F32)
        return carry

    lax.fori_loop(0, here, gather, 0)

    stores = [pltpu.make_async_copy(lw_raw, wg_ref, fetch_sem.at[8])]
    stores[0].start()
    for index, ref in enumerate((qo_ref, ko_ref, vo_ref)):
        for start in range(0, part, chunk):
            fetched[index, pl.ds(start, chunk)] = (
                stage[index, pl.ds(start * heads, chunk * heads), :]
                .reshape(chunk, heads, width)
                .astype(BF16)
            )
            if (start + chunk) % half == 0:
                piece = start // half
                span = pl.ds(piece * half, half)
                copy = pltpu.make_async_copy(
                    fetched.at[index, span], ref.at[span], fetch_sem.at[2 * index + piece]
                )
                copy.start()
                stores.append(copy)
    for copy in stores:
        copy.wait()

    def drain(head, carry):
        for offset in range(1, peers):
            input_copy(head, offset).wait_send()
            output_copy(head, offset).wait_send()
        for offset in range(1, blocks):
            state_copy(head, offset).wait_send()
        return carry

    lax.fori_loop(0, here, drain, 0)


def store_kernel(*refs):
    sources, targets, held, held_levels, sem = refs[:4], refs[4:8], refs[8], refs[9], refs[10]
    part = held.shape[1] // 2
    routes = [(sources[3], held_levels, targets[3])]
    for index in range(3):
        for piece in range(2):
            span = pl.ds(piece * part, part)
            routes.append(
                (sources[index].at[span], held.at[index, span], targets[index].at[span])
            )
    loads = [
        pltpu.make_async_copy(origin, middle, sem.at[0, number])
        for number, (origin, middle, target) in enumerate(routes)
    ]
    stores = [
        pltpu.make_async_copy(middle, target, sem.at[1, number])
        for number, (origin, middle, target) in enumerate(routes)
    ]
    for copy in loads:
        copy.start()
    for load, store in zip(loads, stores):
        load.wait()
        store.start()
    for copy in stores:
        copy.wait()


def on_device(peers, blocks, queries, keys, values, out_grad, level_weights):
    part, heads, width = queries.shape
    here = heads // peers
    toks = part * peers
    far = blocks.bit_length() - 1
    narrow = jax.ShapeDtypeStruct(queries.shape, BF16)
    dma = pltpu.SemaphoreType.DMA
    flops = here * (10 * toks * toks * width + 8 * (far + 2) * toks * width * width)
    hbm = pl.BlockSpec(memory_space=pltpu.HBM)
    turned_levels = jnp.transpose(level_weights, (1, 0, 2))
    shapes = (narrow, narrow, narrow, jax.ShapeDtypeStruct(turned_levels.shape, F32))
    results = pl.pallas_call(
        functools.partial(kernel, peers, blocks),
        out_shape=shapes,
        in_specs=[hbm] * 5,
        out_specs=(hbm,) * 4,
        scratch_shapes=[
            pltpu.VMEM((4, part, heads, width), BF16),
            pltpu.VMEM(turned_levels.shape, F32),
            pltpu.VMEM(level_weights.shape, F32),
            pltpu.VMEM(level_weights.shape, F32),
            pltpu.VMEM((4, part * heads, width), F32),
            pltpu.VMEM((here, peers, 4, part, width), BF16),
            pltpu.VMEM((here, 4, toks, width), BF16),
            pltpu.VMEM((here, 3, toks, width), BF16),
            pltpu.VMEM((here, peers, 3, part, width), BF16),
            pltpu.VMEM((here, far + 1, width, width), BF16),
            pltpu.VMEM((here, blocks, width, width), BF16),
            pltpu.VMEM((toks, toks), F32),
            pltpu.VMEM((toks, toks), F32),
            pltpu.VMEM((toks, toks), BF16),
            pltpu.VMEM((toks, toks), BF16),
            pltpu.VMEM((TILE, TILE), jnp.int32),
            pltpu.VMEM((here, 2, toks, width), F32),
            pltpu.VMEM((here, width, toks), F32),
            pltpu.VMEM((here, 2, width, toks), BF16),
            dma((here, peers)),
            dma((here, peers)),
            dma((here, peers)),
            dma((here, peers)),
            dma((here, blocks)),
            dma((here, blocks)),
            dma((9,)),
        ],
        compiler_params=pltpu.CompilerParams(
            collective_id=0, has_side_effects=True, vmem_limit_bytes=58 * 2**20
        ),
        cost_estimate=pl.CostEstimate(
            flops=flops, bytes_accessed=7 * part * heads * width * 2, transcendentals=0
        ),
    )(queries, keys, values, out_grad, turned_levels)
    stored = pl.pallas_call(
        store_kernel,
        out_shape=shapes,
        in_specs=[hbm] * 4,
        out_specs=(hbm,) * 4,
        scratch_shapes=[
            pltpu.VMEM((3, part, heads, width), BF16),
            pltpu.VMEM(turned_levels.shape, F32),
            dma((2, 7)),
        ],
        compiler_params=pltpu.CompilerParams(vmem_limit_bytes=58 * 2**20),
    )(*results)
    return stored[:3] + (jnp.transpose(stored[3], (1, 0, 2)),)


def solution(mesh):
    wide = P(("seq", "head"), None, None)
    levels = P("head", None, "seq")
    return jax.shard_map(
        functools.partial(on_device, mesh.shape["head"], mesh.shape["seq"]),
        mesh=mesh,
        in_specs=(wide, wide, wide, wide, levels),
        out_specs=(wide, wide, wide, levels),
        check_vma=False,
    )
```
